32 devices in a mesh: dom: 8 (over z, x), blk: 4 (over y, core).
Axes of the slice: x: 2, y: 2, z: 4, core: 2. Of those that a mesh axis runs over, the one named last changes fastest.
Arguments:
- hessian: float32 [32, 15, 192, 192], P('dom')
- neighbours: int32 [32, 15], P('dom'), may hold values from 0 to 31, as said below
- counts: int32 [32], P('dom'), may hold values from 5 to 15
- basis_vectors: float32 [512, 6144], P('blk', 'dom')
Outputs:
- blocks: float32 [2, 64, 6144], P(None, 'blk', 'dom')
- factors: float32 [2, 64, 64], replicated
The draws below stay inside these ranges and needn't reach their ends.
Inputs may be any that keep to these rules, and one draw needn't show every extreme that they name: `neighbours`: entry 0 of tile t's list is t itself; the others are distinct tiles of the domains within two of t's domain, cyclically, where tile t belongs to domain t // 4.
All inputs are finite; a program needn't handle non-finite values.
Results may differ from the reference program's by a relative error of at most 0.00024.
Values sent between devices are 32-bit elements; how exact they have to be, the bound alone decides.
A program may use at most 64 MiB of HBM per device.

```python
import math
import jax
import jax.numpy as jnp
from jax import lax

TILE_ROWS = 192
NEIGHBOURS = 15
BLOCK = 64
STORED = 512
TILES_DEV = 4
N_DOM = 8


def draw_hessian(key, part):
    key_noise, key_diag = jax.random.split(jax.random.fold_in(key, 11))
    full_shape = (TILES_DEV * N_DOM, NEIGHBOURS, TILE_ROWS, TILE_ROWS)
    random_part = jax.random.normal(key_noise, full_shape, jnp.float32)
    random_part = random_part * (NEIGHBOURS * TILE_ROWS) ** (-0.5)
    diag_scale = jnp.exp(jax.random.uniform(key_diag, (TILES_DEV * N_DOM, TILE_ROWS), jnp.float32, 0.0, math.log(4.0)))
    identity = (jnp.arange(TILE_ROWS)[:, None] == jnp.arange(TILE_ROWS)[None, :]).astype(jnp.float32)
    self_block = (jnp.arange(NEIGHBOURS) == 0).astype(jnp.float32)
    return random_part + self_block[None, :, None, None] * diag_scale[:, None, :, None] * identity[None, None, :, :]


def draw_neighbours(key, part):
    tile_total = TILES_DEV * N_DOM
    span = 5 * TILES_DEV
    tile_keys = jax.random.split(jax.random.fold_in(key, 3), tile_total)

    def one_tile(tile_key, tile_id):
        shuffled = jax.random.permutation(tile_key, span - 1)[:NEIGHBOURS - 1]
        own_slot = 2 * TILES_DEV + tile_id % TILES_DEV
        position = jnp.where(shuffled >= own_slot, shuffled + 1, shuffled)
        domain = (tile_id // TILES_DEV + position // TILES_DEV - 2) % N_DOM
        others = domain * TILES_DEV + position % TILES_DEV
        return jnp.concatenate([tile_id[None], others]).astype(jnp.int32)
    return jax.vmap(one_tile)(tile_keys, jnp.arange(tile_total, dtype=jnp.int32))


def draw_counts(key, part):
    tile_total = TILES_DEV * N_DOM
    key_crowd, key_high, key_low = jax.random.split(jax.random.fold_in(key, 5), 3)
    crowded = jax.random.randint(key_crowd, (N_DOM,), 0, 3) == 0
    high_count = jax.random.randint(key_high, (tile_total,), 12, NEIGHBOURS + 1)
    low_count = jax.random.randint(key_low, (tile_total,), 5, 10)
    per_tile = jnp.repeat(crowded, TILES_DEV)
    result = jnp.where(per_tile, high_count, low_count)
    result = result.at[0].set(NEIGHBOURS).at[1].set(5)
    return result.astype(jnp.int32)


def draw_basis_vectors(key, part):
    row_total = TILES_DEV * N_DOM * TILE_ROWS
    normals = jax.random.normal(jax.random.fold_in(key, 7), (STORED + 1, row_total), jnp.float32)
    return (normals[1:] + 0.3 * normals[:-1]) / math.sqrt(1.09)


def setup_inputs(seed: int = 0) -> dict:
    arg_keys = jax.random.split(jax.random.key(seed), 5)
    return {
        "hessian": draw_hessian(jax.random.fold_in(arg_keys[4], 71), 0),
        "neighbours": draw_neighbours(jax.random.fold_in(arg_keys[4], 71), 0),
        "counts": draw_counts(jax.random.fold_in(arg_keys[4], 71), 0),
        "basis_vectors": draw_basis_vectors(jax.random.fold_in(arg_keys[4], 71), 0),
    }


finest = lax.Precision.HIGHEST

def neighbour_product(block_rows, hessian, neighbours, counts):
    col_count = block_rows.shape[0]
    tiled = block_rows.reshape(col_count, -1, TILE_ROWS)
    chosen = tiled[:, neighbours]
    live_mask = (jnp.arange(NEIGHBOURS)[None, :] < counts[:, None]).astype(jnp.float32)
    chosen = chosen * live_mask[None, :, :, None]
    result = jnp.einsum('tkij,btkj->bti', hessian, chosen, precision=finest)
    return result.reshape(col_count, -1)

def reference(hessian, neighbours, counts, basis_vectors):
    row_total = basis_vectors.shape[1]
    stored = basis_vectors
    current = basis_vectors[STORED - BLOCK:]
    blocks = []
    factors = []
    for lanczos_step in range(2):
        pending = neighbour_product(current, hessian, neighbours, counts)
        for sweep_index in range(2):
            coefficients = jnp.dot(stored, pending.T, precision=finest) / row_total
            pending = pending - jnp.dot(coefficients.T, stored, precision=finest)
        gram_block = jnp.dot(pending, pending.T, precision=finest) / row_total
        lower_factor = jnp.linalg.cholesky(gram_block)
        current = jax.scipy.linalg.solve_triangular(lower_factor, pending, lower=True)
        blocks.append(current)
        factors.append(lower_factor.T)
        stored = jnp.concatenate([current, stored[BLOCK:]], axis=0)
    return (jnp.stack(blocks), jnp.stack(factors))
```

```python
import functools

import jax
import jax.numpy as jnp
from jax import lax
from jax.experimental import pallas as pl
from jax.experimental.pallas import tpu as pltpu
from jax.sharding import PartitionSpec as P

BLOCK = 64
STORED = 512
STEPS = 2
SWEEPS = 2
PIECES = 8
SUB, LANE = 8, 128
f32, bf16 = jnp.float32, jnp.bfloat16
finest = lax.Precision.HIGHEST
NT = (((1,), (1,)), ((), ()))
NN = (((1,), (0,)), ((), ()))


def halves(value):
    high = value.astype(bf16)
    return high, (value - high.astype(f32)).astype(bf16)


def stacked(value):
    return jnp.concatenate(halves(value), axis=0)


def folded(double):
    rows = double.shape[0] // 2
    return double[:rows] + double[rows:]


def dot(left, right, dims):
    return lax.dot_general(left, right, dims, preferred_element_type=f32)


def factorize(gram):
    size = gram.shape[0]
    row_id = lax.broadcasted_iota(jnp.int32, (size, size), 0)
    col_id = lax.broadcasted_iota(jnp.int32, (size, size), 1)
    both = jnp.concatenate([gram, (row_id == col_id).astype(f32)], axis=1)
    groups = [both[SUB * g : SUB * g + SUB] for g in range(size // SUB)]
    sub_id = lax.broadcasted_iota(jnp.int32, (SUB, 2 * size), 0)
    for k in range(size):
        g, r = divmod(k, SUB)
        row = groups[g][r : r + 1]
        row = row * (1.0 / row[:, k : k + 1])
        if r < SUB - 1:
            column = groups[g][:, k : k + 1]
            groups[g] = jnp.where(sub_id > r, groups[g] - column * row, groups[g])
        for i in range(g + 1, len(groups)):
            groups[i] = groups[i] - groups[i][:, k : k + 1] * row
    both = jnp.concatenate(groups, axis=0)
    upper = both[:, :size]
    diagonal = jnp.sum(jnp.where(row_id == col_id, upper, 0.0), axis=1, keepdims=True)
    both = both * lax.rsqrt(diagonal)
    return jnp.where(col_id >= row_id, both[:, :size], 0.0), both[:, size:]


def kernel(
    dom_count, blk_count,
    slots_ref, hess_ref, basis_ref,
    blocks_ref, factors_ref,
    hess_f, hess_hi, hess_lo, share_in, ext, ext_b, prod, stored_f, stored_hi, stored_lo,
    part, rs_in, coef, pend, gram_in, new_full,
    hess_sem, x_s, x_r, st_s, st_r, halo_s, halo_r, rs_s, rs_r, ag_s, ag_r, pg_s, pg_r, gr_s, gr_r,
):
    tiles, listed, tile_rows, _ = hess_ref.shape
    per_blk, width = basis_ref.shape
    own = BLOCK // blk_count
    row_total = width * dom_count
    me_d, me_b = lax.axis_index("dom"), lax.axis_index("blk")
    sent = []

    def when(cond, do):
        if cond is None:
            do()
        else:
            pl.when(cond)(do)

    def remote(src, dst, send, recv, target):
        return pltpu.make_async_remote_copy(
            src_ref=src, dst_ref=dst, send_sem=send, recv_sem=recv,
            device_id=target, device_id_type=pl.DeviceIdType.MESH,
        )

    def send(cond, *what):
        copy = remote(*what)
        when(cond, copy.start)
        sent.append((cond, copy))

    for t in range(tiles):
        pltpu.make_async_copy(hess_ref.at[t], hess_f.at[t], hess_sem.at[t]).start()

    def dom_peer(o):
        return lax.rem(me_d + o + dom_count, dom_count)

    def blk_peer(o):
        return lax.rem(me_b + o + blk_count, blk_count)

    barrier = pltpu.get_barrier_semaphore()
    for o in range(1, dom_count):
        pl.semaphore_signal(barrier, inc=1, device_id=(dom_peer(o), me_b), device_id_type=pl.DeviceIdType.MESH)
    for o in range(1, blk_count):
        pl.semaphore_signal(barrier, inc=1, device_id=(me_d, blk_peer(o)), device_id_type=pl.DeviceIdType.MESH)
    pl.semaphore_wait(barrier, dom_count + blk_count - 2)

    last = blk_count - 1
    for j in range(last):
        rows = basis_ref.at[pl.ds(per_blk - BLOCK + own * j, own)]
        send(me_b == last, rows, share_in, x_s.at[j], x_r, (me_d, j))

    partner = me_b + 1 - 2 * lax.rem(me_b, 2)
    across = lax.rem(me_b + 2, 4)
    send(None, basis_ref, stored_f.at[me_b], st_s.at[0], st_r.at[0], (me_d, across))
    send(None, basis_ref, stored_f.at[me_b], st_s.at[1], st_r.at[1], (me_d, partner))
    stored_f[me_b] = basis_ref[...]

    @pl.when(me_b == last)
    def _():
        share_in[...] = basis_ref[per_blk - own :, :]

    @pl.when(me_b != last)
    def _():
        remote(share_in, share_in, x_s.at[0], x_r, (me_d, last)).wait_recv()

    def start_halo(step, share):
        for t in range(tiles):
            ext[step, 2, t] = share[:, t * tile_rows : (t + 1) * tile_rows]
        for i, o in enumerate((2, -2, 1, -1)):
            send(None, ext.at[step, 2], ext.at[step, 2 - o], halo_s.at[step, i], halo_r.at[step, i], (dom_peer(o), me_b))

    def split_ext(step, i):
        for t in range(tiles):
            ext_b[i * tiles + t] = stacked(ext[step, i, t])

    def end_halo(step):
        split_ext(step, 2)
        for i, o in enumerate((2, -2, 1, -1)):
            remote(ext.at[step, 2], ext.at[step, 2 - o], halo_s.at[step, i], halo_r.at[step, i], (dom_peer(-o), me_b)).wait_recv()
            split_ext(step, 2 - o)

    def product():
        @pl.loop(0, tiles)
        def _(t):
            total = jnp.zeros((2 * own, tile_rows), f32)
            for k in range(listed):
                x = ext_b[slots_ref[t * listed + k]]
                total += dot(x, hess_hi[t, k], NT) + dot(x, hess_lo[t, k], NT)
            prod[t] = folded(total)

        return jnp.concatenate([prod[t] for t in range(tiles)], axis=1)

    def summed(a, value):
        lanes = STORED // LANE
        for j in range(PIECES):
            h, q = divmod(j, lanes)
            part[a, j] = value[h * SUB : (h + 1) * SUB, q * LANE : (q + 1) * LANE]
        all_own = dom_count <= PIECES
        for o in range(1, dom_count):
            to = dom_peer(o)
            cond = None if all_own else to < PIECES
            piece = to if all_own else lax.rem(to, PIECES)
            send(cond, part.at[a, piece], rs_in.at[a, o], rs_s.at[a, o], rs_r.at[a, o], (to, me_b))
        mine = me_d if all_own else lax.rem(me_d, PIECES)
        owner = None if all_own else me_d < PIECES

        def reduce():
            total = part[a, mine]
            for o in range(1, dom_count):
                remote(part.at[a, 0], rs_in.at[a, o], rs_s.at[a, o], rs_r.at[a, o], (dom_peer(-o), me_b)).wait_recv()
                total += rs_in[a, o]
            coef[a, mine] = total / row_total

        when(owner, reduce)
        for o in range(1, dom_count):
            send(owner, coef.at[a, mine], coef.at[a, mine], ag_s.at[a, o], ag_r.at[a, o], (dom_peer(o), me_b))
        for o in range(1, dom_count):
            origin = dom_peer(-o)
            cond = None if all_own else origin < PIECES
            copy = remote(coef.at[a, 0], coef.at[a, 0], ag_s.at[a, o], ag_r.at[a, o], (origin, me_b))
            when(cond, copy.wait_recv)
        return jnp.concatenate(
            [jnp.concatenate([coef[a, h * lanes + q] for q in range(lanes)], axis=1) for h in range(PIECES // lanes)], axis=0
        )

    start_halo(0, share_in[...])
    ext_b[5 * tiles] = jnp.zeros(ext_b.shape[1:], bf16)
    for t in range(tiles):
        pltpu.make_async_copy(hess_ref.at[t], hess_f.at[t], hess_sem.at[t]).wait()

        @pl.loop(0, listed)
        def _(k):
            high, low = halves(hess_f[t, k])
            hess_hi[t, k] = high
            hess_lo[t, k] = low

    for step in range(STEPS):
        end_halo(step)
        pending = product()
        if step == 0:
            remote(basis_ref, stored_f.at[0], st_s.at[0], st_r.at[0], (me_d, across)).wait_recv()
            send(None, stored_f.at[across], stored_f.at[across], st_s.at[2], st_r.at[2], (me_d, partner))
            for i in (1, 2):
                remote(basis_ref, stored_f.at[0], st_s.at[i], st_r.at[i], (me_d, partner)).wait_recv()
            for i in range(blk_count):
                high, low = halves(stored_f[i])
                stored_hi[i * per_blk : (i + 1) * per_blk] = high
                stored_lo[i * per_blk : (i + 1) * per_blk] = low
        for sweep in range(SWEEPS):
            both = stacked(pending)
            inner = folded(dot(both, stored_hi[...], NT) + dot(both, stored_lo[...], NT))
            both = stacked(summed(SWEEPS * step + sweep, inner))
            pending = pending - folded(dot(both, stored_hi[...], NN) + dot(both, stored_lo[...], NN))
        pend[step, me_b] = pending
        for o in range(1, blk_count):
            send(None, pend.at[step, me_b], pend.at[step, me_b], pg_s.at[step, o], pg_r.at[step, o], (me_d, blk_peer(o)))
        for o in range(1, blk_count):
            remote(pend.at[step, 0], pend.at[step, 0], pg_s.at[step, o], pg_r.at[step, o], (me_d, blk_peer(-o))).wait_recv()
        full = jnp.concatenate([pend[step, i] for i in range(blk_count)], axis=0)
        high, low = halves(full)
        cross = dot(high, low, NT)
        gram_part = dot(high, high, NT) + cross + cross.T
        half = BLOCK // 2
        gram_in[step, me_d] = jnp.concatenate([gram_part[:half], gram_part[half:]], axis=1)
        for o in range(1, dom_count):
            send(None, gram_in.at[step, me_d], gram_in.at[step, me_d], gr_s.at[step, o], gr_r.at[step, o], (dom_peer(o), me_b))
        for o in range(1, dom_count):
            remote(gram_in.at[step, 0], gram_in.at[step, 0], gr_s.at[step, o], gr_r.at[step, o], (dom_peer(-o), me_b)).wait_recv()
        total = gram_in[step, 0]
        for d in range(1, dom_count):
            total += gram_in[step, d]
        total = total / row_total
        gram = jnp.concatenate([total[:, :BLOCK], total[:, BLOCK:]], axis=0)
        upper, inverse = factorize(gram)
        factors_ref[step] = upper
        new = lax.dot_general(inverse, full, NN, precision=finest, preferred_element_type=f32)
        new_full[step] = new
        share = new_full[step, pl.ds(pl.multiple_of(me_b * own, own), own), :]
        blocks_ref[step] = share
        if step + 1 < STEPS:
            start_halo(step + 1, share)
            high, low = halves(new)
            stored_hi[:BLOCK] = high
            stored_lo[:BLOCK] = low

    for cond, copy in sent:
        when(cond, copy.wait_send)


def local(hessian, neighbours, counts, basis_vectors):
    dom_count = lax.axis_size("dom")
    blk_count = lax.axis_size("blk")
    me_dom = lax.axis_index("dom")
    tiles, listed, tile_rows, _ = hessian.shape
    per_blk, width = basis_vectors.shape
    own = BLOCK // blk_count
    slot = (neighbours // tiles - me_dom + 2) % dom_count * tiles + neighbours % tiles
    live = jnp.arange(listed)[None, :] < counts[:, None]
    slots = jnp.where(live, slot, 5 * tiles).reshape(-1).astype(jnp.int32)
    sums = STEPS * SWEEPS
    dma = pltpu.SemaphoreType.DMA
    vmem = pl.BlockSpec(memory_space=pltpu.VMEM)
    return pl.pallas_call(
        functools.partial(kernel, dom_count, blk_count),
        out_shape=(
            jax.ShapeDtypeStruct((STEPS, own, width), f32),
            jax.ShapeDtypeStruct((STEPS, BLOCK, BLOCK), f32),
        ),
        in_specs=[pl.BlockSpec(memory_space=pltpu.SMEM), pl.BlockSpec(memory_space=pl.ANY), vmem],
        out_specs=(vmem, vmem),
        scratch_shapes=[
            pltpu.VMEM(hessian.shape, f32),
            pltpu.VMEM(hessian.shape, bf16),
            pltpu.VMEM(hessian.shape, bf16),
            pltpu.VMEM((own, width), f32),
            pltpu.VMEM((STEPS, 5, tiles, own, tile_rows), f32),
            pltpu.VMEM((5 * tiles + 1, 2 * own, tile_rows), bf16),
            pltpu.VMEM((tiles, own, tile_rows), f32),
            pltpu.VMEM((blk_count, per_blk, width), f32),
            pltpu.VMEM((STORED, width), bf16),
            pltpu.VMEM((STORED, width), bf16),
            pltpu.VMEM((sums, PIECES, SUB, LANE), f32),
            pltpu.VMEM((sums, dom_count, SUB, LANE), f32),
            pltpu.VMEM((sums, PIECES, SUB, LANE), f32),
            pltpu.VMEM((STEPS, blk_count, own, width), f32),
            pltpu.VMEM((STEPS, dom_count, BLOCK // 2, 2 * BLOCK), f32),
            pltpu.VMEM((STEPS, BLOCK, width), f32),
            dma((tiles,)),
            dma((blk_count,)), dma,
            dma((3,)), dma((3,)),
            dma((STEPS, 4)), dma((STEPS, 4)),
            dma((sums, dom_count)), dma((sums, dom_count)),
            dma((sums, dom_count)), dma((sums, dom_count)),
            dma((STEPS, blk_count)), dma((STEPS, blk_count)),
            dma((STEPS, dom_count)), dma((STEPS, dom_count)),
        ],
        compiler_params=pltpu.CompilerParams(
            collective_id=0, has_side_effects=True, vmem_limit_bytes=56 * 1024 * 1024
        ),
        name="lanczos",
    )(slots, hessian, basis_vectors)


def solution(mesh):
    placed = (P("dom", None, None, None), P("dom", None), P("dom"), P("blk", "dom"))
    return jax.shard_map(
        local, mesh=mesh, in_specs=placed, out_specs=(P(None, "blk", "dom"), P()), check_vma=False
    )
```

```python
import functools

import jax
import jax.numpy as jnp
from jax import lax
from jax.experimental import pallas as pl
from jax.experimental.pallas import tpu as pltpu
from jax.sharding import PartitionSpec as P

BLOCK = 64
STORED = 512
STEPS = 2
SWEEPS = 2
PIECES = 8
SUB, LANE = 8, 128
f32, bf16 = jnp.float32, jnp.bfloat16
finest = lax.Precision.HIGHEST
NT = (((1,), (1,)), ((), ()))
NN = (((1,), (0,)), ((), ()))


def halves(value):
    high = value.astype(bf16)
    return high, (value - high.astype(f32)).astype(bf16)


def stacked(value):
    return jnp.concatenate(halves(value), axis=0)


def folded(double):
    rows = double.shape[0] // 2
    return double[:rows] + double[rows:]


def dot(left, right, dims):
    return lax.dot_general(left, right, dims, preferred_element_type=f32)


def factorize(gram):
    size = gram.shape[0]
    row_id = lax.broadcasted_iota(jnp.int32, (size, size), 0)
    col_id = lax.broadcasted_iota(jnp.int32, (size, size), 1)
    both = jnp.concatenate([gram, (row_id == col_id).astype(f32)], axis=1)
    groups = [both[SUB * g : SUB * g + SUB] for g in range(size // SUB)]
    sub_id = lax.broadcasted_iota(jnp.int32, (SUB, 2 * size), 0)
    spread = (SUB, 2 * size)
    for k in range(0, size, 2):
        g, r = divmod(k, SUB)
        first = {i: jnp.broadcast_to(groups[i][:, k : k + 1], spread) for i in range(g, len(groups))}
        second = {i: jnp.broadcast_to(groups[i][:, k + 1 : k + 2], spread) for i in range(g, len(groups))}
        row0, row1 = groups[g][r : r + 1], groups[g][r + 1 : r + 2]
        inverse0 = 1.0 / first[g][r : r + 1]
        below = first[g][r + 1 : r + 2]
        scale = below * inverse0
        inverse1 = 1.0 / (second[g][r + 1 : r + 2] - scale * below)
        row1 = row1 - scale * row0
        solved1 = row1 * inverse1
        solved0 = row0 * inverse0 - scale * solved1
        for i in range(g, len(groups)):
            rest = groups[i] - first[i] * solved0 - second[i] * solved1
            if i == g:
                rest = jnp.where(sub_id > r + 1, rest, jnp.where(sub_id == r + 1, row1, groups[i]))
            groups[i] = rest
    both = jnp.concatenate(groups, axis=0)
    upper = both[:, :size]
    diagonal = jnp.sum(jnp.where(row_id == col_id, upper, 0.0), axis=1, keepdims=True)
    both = both * lax.rsqrt(diagonal)
    return jnp.where(col_id >= row_id, both[:, :size], 0.0), both[:, size:]


def kernel(
    dom_count, blk_count,
    slots_ref, hess_ref, basis_ref,
    blocks_ref, factors_ref,
    hess_f, hess_hi, hess_lo, share_in, ext, ext_b, prod, stored_f, stored_hi, stored_lo,
    part, rs_in, coef, pend, gram_in, new_full,
    hess_sem, x_s, x_r, st_s, st_r, halo_s, halo_r, rs_s, rs_r, ag_s, ag_r, pg_s, pg_r, gr_s, gr_r,
):
    tiles, listed, tile_rows, _ = hess_ref.shape
    per_blk, width = basis_ref.shape
    own = BLOCK // blk_count
    row_total = width * dom_count
    me_d, me_b = lax.axis_index("dom"), lax.axis_index("blk")
    sent = []

    def when(cond, do):
        if cond is None:
            do()
        else:
            pl.when(cond)(do)

    def remote(src, dst, send, recv, target):
        return pltpu.make_async_remote_copy(
            src_ref=src, dst_ref=dst, send_sem=send, recv_sem=recv,
            device_id=target, device_id_type=pl.DeviceIdType.MESH,
        )

    def send(cond, *what):
        copy = remote(*what)
        when(cond, copy.start)
        sent.append((cond, copy))

    for t in range(tiles):
        pltpu.make_async_copy(hess_ref.at[t], hess_f.at[t], hess_sem.at[t]).start()

    def dom_peer(o):
        return lax.rem(me_d + o + dom_count, dom_count)

    def blk_peer(o):
        return lax.rem(me_b + o + blk_count, blk_count)

    barrier = pltpu.get_barrier_semaphore()
    for o in range(1, dom_count):
        pl.semaphore_signal(barrier, inc=1, device_id=(dom_peer(o), me_b), device_id_type=pl.DeviceIdType.MESH)
    for o in range(1, blk_count):
        pl.semaphore_signal(barrier, inc=1, device_id=(me_d, blk_peer(o)), device_id_type=pl.DeviceIdType.MESH)
    pl.semaphore_wait(barrier, dom_count + blk_count - 2)

    last = blk_count - 1
    for j in range(last):
        rows = basis_ref.at[pl.ds(per_blk - BLOCK + own * j, own)]
        send(me_b == last, rows, share_in, x_s.at[j], x_r, (me_d, j))

    partner = me_b + 1 - 2 * lax.rem(me_b, 2)
    across = lax.rem(me_b + 2, 4)
    send(None, basis_ref, stored_f.at[me_b], st_s.at[0], st_r.at[0], (me_d, across))
    send(None, basis_ref, stored_f.at[me_b], st_s.at[1], st_r.at[1], (me_d, partner))
    stored_f[me_b] = basis_ref[...]

    @pl.when(me_b == last)
    def _():
        share_in[...] = basis_ref[per_blk - own :, :]

    @pl.when(me_b != last)
    def _():
        remote(share_in, share_in, x_s.at[0], x_r, (me_d, last)).wait_recv()

    def start_halo(step, share):
        for t in range(tiles):
            ext[step, 2, t] = share[:, t * tile_rows : (t + 1) * tile_rows]
        for i, o in enumerate((2, -2, 1, -1)):
            send(None, ext.at[step, 2], ext.at[step, 2 - o], halo_s.at[step, i], halo_r.at[step, i], (dom_peer(o), me_b))

    def split_ext(step, i):
        for t in range(tiles):
            ext_b[i * tiles + t] = stacked(ext[step, i, t])

    def end_halo(step):
        split_ext(step, 2)
        for i, o in enumerate((2, -2, 1, -1)):
            remote(ext.at[step, 2], ext.at[step, 2 - o], halo_s.at[step, i], halo_r.at[step, i], (dom_peer(-o), me_b)).wait_recv()
            split_ext(step, 2 - o)

    def product(first, end):
        @pl.loop(first, end)
        def _(t):
            total = jnp.zeros((tile_rows, 2 * own), f32)
            for k in range(listed):
                x = ext_b[slots_ref[t * listed + k]]
                total += dot(hess_hi[t, k], x, NT) + dot(hess_lo[t, k], x, NT)
            prod[t] = folded(total.T)

    def split_stored(i):
        high, low = halves(stored_f[i])
        rows = pl.ds(pl.multiple_of(i * per_blk, per_blk), per_blk)
        stored_hi[rows] = high
        stored_lo[rows] = low

    def summed(a, value):
        lanes = STORED // LANE
        for j in range(PIECES):
            h, q = divmod(j, lanes)
            part[a, j] = value[h * SUB : (h + 1) * SUB, q * LANE : (q + 1) * LANE]
        all_own = dom_count <= PIECES
        for o in range(1, dom_count):
            to = dom_peer(o)
            cond = None if all_own else to < PIECES
            piece = to if all_own else lax.rem(to, PIECES)
            send(cond, part.at[a, piece], rs_in.at[a, o], rs_s.at[a, o], rs_r.at[a, o], (to, me_b))
        mine = me_d if all_own else lax.rem(me_d, PIECES)
        owner = None if all_own else me_d < PIECES

        def reduce():
            total = part[a, mine]
            for o in range(1, dom_count):
                remote(part.at[a, 0], rs_in.at[a, o], rs_s.at[a, o], rs_r.at[a, o], (dom_peer(-o), me_b)).wait_recv()
                total += rs_in[a, o]
            coef[a, mine] = total / row_total

        when(owner, reduce)
        for o in range(1, dom_count):
            send(owner, coef.at[a, mine], coef.at[a, mine], ag_s.at[a, o], ag_r.at[a, o], (dom_peer(o), me_b))
        for o in range(1, dom_count):
            origin = dom_peer(-o)
            cond = None if all_own else origin < PIECES
            copy = remote(coef.at[a, 0], coef.at[a, 0], ag_s.at[a, o], ag_r.at[a, o], (origin, me_b))
            when(cond, copy.wait_recv)
        return jnp.concatenate(
            [jnp.concatenate([coef[a, h * lanes + q] for q in range(lanes)], axis=1) for h in range(PIECES // lanes)], axis=0
        )

    start_halo(0, share_in[...])
    ext_b[5 * tiles] = jnp.zeros(ext_b.shape[1:], bf16)
    for t in range(tiles):
        pltpu.make_async_copy(hess_ref.at[t], hess_f.at[t], hess_sem.at[t]).wait()

        @pl.loop(0, listed)
        def _(k):
            high, low = halves(hess_f[t, k])
            hess_hi[t, k] = high
            hess_lo[t, k] = low

    split_stored(me_b)
    for step in range(STEPS):
        end_halo(step)
        product(0, tiles // 2)
        if step == 0:
            remote(basis_ref, stored_f.at[0], st_s.at[0], st_r.at[0], (me_d, across)).wait_recv()
            send(None, stored_f.at[across], stored_f.at[across], st_s.at[2], st_r.at[2], (me_d, partner))
        product(tiles // 2, tiles)
        pending = jnp.concatenate([prod[t] for t in range(tiles)], axis=1)
        if step == 0:
            split_stored(across)
            for i, origin in ((1, partner), (2, lax.rem(partner + 2, 4))):
                remote(basis_ref, stored_f.at[0], st_s.at[i], st_r.at[i], (me_d, partner)).wait_recv()
                split_stored(origin)
        for sweep in range(SWEEPS):
            both = stacked(pending)
            inner = folded((dot(stored_hi[...], both, NT) + dot(stored_lo[...], both, NT)).T)
            both = stacked(summed(SWEEPS * step + sweep, inner))
            pending = pending - folded(dot(both, stored_hi[...], NN) + dot(both, stored_lo[...], NN))
        pend[step, me_b] = pending
        for o in range(1, blk_count):
            send(None, pend.at[step, me_b], pend.at[step, me_b], pg_s.at[step, o], pg_r.at[step, o], (me_d, blk_peer(o)))
        for o in range(1, blk_count):
            remote(pend.at[step, 0], pend.at[step, 0], pg_s.at[step, o], pg_r.at[step, o], (me_d, blk_peer(-o))).wait_recv()
        full = jnp.concatenate([pend[step, i] for i in range(blk_count)], axis=0)
        high, low = halves(full)
        cross = dot(high, low, NT)
        gram_part = dot(high, high, NT) + cross + cross.T
        half = BLOCK // 2
        gram_in[step, me_d] = jnp.concatenate([gram_part[:half], gram_part[half:]], axis=1)
        for o in range(1, dom_count):
            send(None, gram_in.at[step, me_d], gram_in.at[step, me_d], gr_s.at[step, o], gr_r.at[step, o], (dom_peer(o), me_b))
        for o in range(1, dom_count):
            remote(gram_in.at[step, 0], gram_in.at[step, 0], gr_s.at[step, o], gr_r.at[step, o], (dom_peer(-o), me_b)).wait_recv()
        total = gram_in[step, 0]
        for d in range(1, dom_count):
            total += gram_in[step, d]
        total = total / row_total
        gram = jnp.concatenate([total[:, :BLOCK], total[:, BLOCK:]], axis=0)
        upper, inverse = factorize(gram)
        factors_ref[step] = upper
        new = lax.dot_general(inverse, full, NN, precision=finest, preferred_element_type=f32)
        new_full[step] = new
        share = new_full[step, pl.ds(pl.multiple_of(me_b * own, own), own), :]
        blocks_ref[step] = share
        if step + 1 < STEPS:
            start_halo(step + 1, share)
            high, low = halves(new)
            stored_hi[:BLOCK] = high
            stored_lo[:BLOCK] = low

    for cond, copy in sent:
        when(cond, copy.wait_send)


def local(hessian, neighbours, counts, basis_vectors):
    dom_count = lax.axis_size("dom")
    blk_count = lax.axis_size("blk")
    me_dom = lax.axis_index("dom")
    tiles, listed, tile_rows, _ = hessian.shape
    per_blk, width = basis_vectors.shape
    own = BLOCK // blk_count
    slot = (neighbours // tiles - me_dom + 2) % dom_count * tiles + neighbours % tiles
    live = jnp.arange(listed)[None, :] < counts[:, None]
    slots = jnp.where(live, slot, 5 * tiles).reshape(-1).astype(jnp.int32)
    sums = STEPS * SWEEPS
    dma = pltpu.SemaphoreType.DMA
    vmem = pl.BlockSpec(memory_space=pltpu.VMEM)
    return pl.pallas_call(
        functools.partial(kernel, dom_count, blk_count),
        out_shape=(
            jax.ShapeDtypeStruct((STEPS, own, width), f32),
            jax.ShapeDtypeStruct((STEPS, BLOCK, BLOCK), f32),
        ),
        in_specs=[pl.BlockSpec(memory_space=pltpu.SMEM), pl.BlockSpec(memory_space=pl.ANY), vmem],
        out_specs=(vmem, vmem),
        scratch_shapes=[
            pltpu.VMEM(hessian.shape, f32),
            pltpu.VMEM(hessian.shape, bf16),
            pltpu.VMEM(hessian.shape, bf16),
            pltpu.VMEM((own, width), f32),
            pltpu.VMEM((STEPS, 5, tiles, own, tile_rows), f32),
            pltpu.VMEM((5 * tiles + 1, 2 * own, tile_rows), bf16),
            pltpu.VMEM((tiles, own, tile_rows), f32),
            pltpu.VMEM((blk_count, per_blk, width), f32),
            pltpu.VMEM((STORED, width), bf16),
            pltpu.VMEM((STORED, width), bf16),
            pltpu.VMEM((sums, PIECES, SUB, LANE), f32),
            pltpu.VMEM((sums, dom_count, SUB, LANE), f32),
            pltpu.VMEM((sums, PIECES, SUB, LANE), f32),
            pltpu.VMEM((STEPS, blk_count, own, width), f32),
            pltpu.VMEM((STEPS, dom_count, BLOCK // 2, 2 * BLOCK), f32),
            pltpu.VMEM((STEPS, BLOCK, width), f32),
            dma((tiles,)),
            dma((blk_count,)), dma,
            dma((3,)), dma((3,)),
            dma((STEPS, 4)), dma((STEPS, 4)),
            dma((sums, dom_count)), dma((sums, dom_count)),
            dma((sums, dom_count)), dma((sums, dom_count)),
            dma((STEPS, blk_count)), dma((STEPS, blk_count)),
            dma((STEPS, dom_count)), dma((STEPS, dom_count)),
        ],
        compiler_params=pltpu.CompilerParams(
            collective_id=0, has_side_effects=True, vmem_limit_bytes=56 * 1024 * 1024
        ),
        name="lanczos",
    )(slots, hessian, basis_vectors)


def solution(mesh):
    placed = (P("dom", None, None, None), P("dom", None), P("dom"), P("blk", "dom"))
    return jax.shard_map(
        local, mesh=mesh, in_specs=placed, out_specs=(P(None, "blk", "dom"), P()), check_vma=False
    )
```

```python
import functools

import jax
import jax.numpy as jnp
from jax import lax
from jax.experimental import pallas as pl
from jax.experimental.pallas import tpu as pltpu
from jax.sharding import PartitionSpec as P

BLOCK = 64
STORED = 512
STEPS = 2
SWEEPS = 2
PIECES = 8
SUB, LANE = 8, 128
f32, bf16 = jnp.float32, jnp.bfloat16
finest = lax.Precision.HIGHEST
NT = (((1,), (1,)), ((), ()))
NN = (((1,), (0,)), ((), ()))


def halves(value):
    high = value.astype(bf16)
    return high, (value - high.astype(f32)).astype(bf16)


def stacked(value):
    return jnp.concatenate(halves(value), axis=0)


def folded(double):
    rows = double.shape[0] // 2
    return double[:rows] + double[rows:]


def dot(left, right, dims):
    return lax.dot_general(left, right, dims, preferred_element_type=f32)


def factorize(gram):
    size = gram.shape[0]
    row_id = lax.broadcasted_iota(jnp.int32, (size, size), 0)
    col_id = lax.broadcasted_iota(jnp.int32, (size, size), 1)
    both = jnp.concatenate([gram, (row_id == col_id).astype(f32)], axis=1)
    groups = [both[SUB * g : SUB * g + SUB] for g in range(size // SUB)]
    sub_id = lax.broadcasted_iota(jnp.int32, (SUB, 2 * size), 0)
    spread = (SUB, 2 * size)
    for k in range(0, size, 2):
        g, r = divmod(k, SUB)
        first = {i: jnp.broadcast_to(groups[i][:, k : k + 1], spread) for i in range(g, len(groups))}
        second = {i: jnp.broadcast_to(groups[i][:, k + 1 : k + 2], spread) for i in range(g, len(groups))}
        row0, row1 = groups[g][r : r + 1], groups[g][r + 1 : r + 2]
        inverse0 = 1.0 / first[g][r : r + 1]
        below = first[g][r + 1 : r + 2]
        scale = below * inverse0
        inverse1 = 1.0 / (second[g][r + 1 : r + 2] - scale * below)
        row1 = row1 - scale * row0
        solved1 = row1 * inverse1
        solved0 = row0 * inverse0 - scale * solved1
        for i in range(g, len(groups)):
            rest = groups[i] - first[i] * solved0 - second[i] * solved1
            if i == g:
                rest = jnp.where(sub_id > r + 1, rest, jnp.where(sub_id == r + 1, row1, groups[i]))
            groups[i] = rest
    both = jnp.concatenate(groups, axis=0)
    upper = both[:, :size]
    diagonal = jnp.sum(jnp.where(row_id == col_id, upper, 0.0), axis=1, keepdims=True)
    both = both * lax.rsqrt(diagonal)
    return jnp.where(col_id >= row_id, both[:, :size], 0.0), both[:, size:]


def kernel(
    dom_count, blk_count,
    slots_ref, hess_ref, basis_ref,
    blocks_ref, factors_ref,
    hess_f, hess_hi, hess_lo, share_in, ext, ext_b, prod, stored_f, stored_hi, stored_lo,
    part, rs_in, coef, pend, gram_in, new_full, own_coef, mat_part, mat_in, mat_all, mat, mat_hi, mat_lo,
    hess_sem, x_s, x_r, st_s, st_r, halo_s, halo_r, rs_s, rs_r, ag_s, ag_r, pg_s, pg_r, gr_s, gr_r,
    cg_s, cg_r, ms_s, ms_r, mg_s, mg_r, mb_s, mb_r,
):
    tiles, listed, tile_rows, _ = hess_ref.shape
    per_blk, width = basis_ref.shape
    own = BLOCK // blk_count
    row_total = width * dom_count
    me_d, me_b = lax.axis_index("dom"), lax.axis_index("blk")
    sent = []

    def when(cond, do):
        if cond is None:
            do()
        else:
            pl.when(cond)(do)

    def remote(src, dst, send, recv, target):
        return pltpu.make_async_remote_copy(
            src_ref=src, dst_ref=dst, send_sem=send, recv_sem=recv,
            device_id=target, device_id_type=pl.DeviceIdType.MESH,
        )

    def send(cond, *what):
        copy = remote(*what)
        when(cond, copy.start)
        sent.append((cond, copy))

    for t in range(tiles):
        pltpu.make_async_copy(hess_ref.at[t], hess_f.at[t], hess_sem.at[t]).start()

    def dom_peer(o):
        return lax.rem(me_d + o + dom_count, dom_count)

    def blk_peer(o):
        return lax.rem(me_b + o + blk_count, blk_count)

    barrier = pltpu.get_barrier_semaphore()
    for o in range(1, dom_count):
        pl.semaphore_signal(barrier, inc=1, device_id=(dom_peer(o), me_b), device_id_type=pl.DeviceIdType.MESH)
    for o in range(1, blk_count):
        pl.semaphore_signal(barrier, inc=1, device_id=(me_d, blk_peer(o)), device_id_type=pl.DeviceIdType.MESH)
    pl.semaphore_wait(barrier, dom_count + blk_count - 2)

    last = blk_count - 1
    for j in range(last):
        rows = basis_ref.at[pl.ds(per_blk - BLOCK + own * j, own)]
        send(me_b == last, rows, share_in, x_s.at[j], x_r, (me_d, j))

    partner = me_b + 1 - 2 * lax.rem(me_b, 2)
    across = lax.rem(me_b + 2, 4)
    send(None, basis_ref, stored_f.at[me_b], st_s.at[0], st_r.at[0], (me_d, across))
    send(None, basis_ref, stored_f.at[me_b], st_s.at[1], st_r.at[1], (me_d, partner))
    stored_f[me_b] = basis_ref[...]

    @pl.when(me_b == last)
    def _():
        share_in[...] = basis_ref[per_blk - own :, :]

    @pl.when(me_b != last)
    def _():
        remote(share_in, share_in, x_s.at[0], x_r, (me_d, last)).wait_recv()

    def start_halo(step, share):
        for t in range(tiles):
            ext[step, 2, t] = share[:, t * tile_rows : (t + 1) * tile_rows]
        for i, o in enumerate((2, -2, 1, -1)):
            send(None, ext.at[step, 2], ext.at[step, 2 - o], halo_s.at[step, i], halo_r.at[step, i], (dom_peer(o), me_b))

    def split_ext(step, i):
        for t in range(tiles):
            ext_b[i * tiles + t] = stacked(ext[step, i, t])

    def end_halo(step):
        split_ext(step, 2)
        for i, o in enumerate((2, -2, 1, -1)):
            remote(ext.at[step, 2], ext.at[step, 2 - o], halo_s.at[step, i], halo_r.at[step, i], (dom_peer(-o), me_b)).wait_recv()
            split_ext(step, 2 - o)

    def product(first, end):
        @pl.loop(first, end)
        def _(t):
            total = jnp.zeros((tile_rows, 2 * own), f32)
            for k in range(listed):
                x = ext_b[slots_ref[t * listed + k]]
                total += dot(hess_hi[t, k], x, NT) + dot(hess_lo[t, k], x, NT)
            prod[t] = folded(total.T)

    def split_stored(i):
        high, low = halves(stored_f[i])
        rows = pl.ds(pl.multiple_of(i * per_blk, per_blk), per_blk)
        stored_hi[rows] = high
        stored_lo[rows] = low

    all_own = dom_count <= PIECES
    mine = me_d if all_own else lax.rem(me_d, PIECES)
    owner = None if all_own else me_d < PIECES

    def scatter_mat():
        rows = pl.ds(pl.multiple_of(me_b * per_blk, per_blk), per_blk)
        high, low = stored_hi[rows], stored_lo[rows]
        value = dot(high, stored_hi[...], NT) + dot(high, stored_lo[...], NT) + dot(low, stored_hi[...], NT)
        each = per_blk // PIECES
        for j in range(PIECES):
            mat_part[j] = value[j * each : (j + 1) * each]
        for o in range(1, dom_count):
            to = dom_peer(o)
            cond = None if all_own else to < PIECES
            piece = to if all_own else lax.rem(to, PIECES)
            send(cond, mat_part.at[piece], mat_in.at[o], ms_s.at[o], ms_r.at[o], (to, me_b))

    def reduce_mat():
        def reduce():
            total = mat_part[mine]
            for o in range(1, dom_count):
                remote(mat_part.at[0], mat_in.at[o], ms_s.at[o], ms_r.at[o], (dom_peer(-o), me_b)).wait_recv()
                total += mat_in[o]
            mat_all[me_b, mine] = total / row_total

        when(owner, reduce)
        for o in range(1, dom_count):
            piece = mat_all.at[me_b, mine]
            send(owner, piece, piece, mg_s.at[o], mg_r.at[o], (dom_peer(o), me_b))

    def spread_mat():
        for o in range(1, dom_count):
            origin = dom_peer(-o)
            cond = None if all_own else origin < PIECES
            piece = mat_all.at[me_b, 0]
            when(cond, remote(piece, piece, mg_s.at[o], mg_r.at[o], (origin, me_b)).wait_recv)
        for o in range(1, blk_count):
            send(None, mat_all.at[me_b], mat_all.at[me_b], mb_s.at[o], mb_r.at[o], (me_d, blk_peer(o)))

    def times_mat(value):
        both = stacked(value)
        return folded(dot(both, mat_hi[...], NN) + dot(both, mat_lo[...], NN))

    def split_mat():
        high, low = halves(mat[...])
        mat_hi[...] = high
        mat_lo[...] = low

    def replace_mat(inverse):
        for o in range(1, blk_count):
            remote(mat_all.at[0], mat_all.at[0], mb_s.at[o], mb_r.at[o], (me_d, blk_peer(-o))).wait_recv()
        each = per_blk // PIECES
        for i in range(blk_count):
            for j in range(PIECES):
                mat[i * per_blk + j * each : i * per_blk + (j + 1) * each] = mat_all[i, j]
        split_mat()
        second = all_coef(0)
        rows = lax.dot_general(
            inverse, second - times_mat(second), NN, precision=finest, preferred_element_type=f32
        )
        mat[:, : 2 * BLOCK] = jnp.concatenate([rows.T, mat[:, BLOCK : 2 * BLOCK]], axis=1)
        unit = lax.broadcasted_iota(jnp.int32, (BLOCK, BLOCK), 0) == lax.broadcasted_iota(jnp.int32, (BLOCK, BLOCK), 1)
        mat[:BLOCK] = jnp.concatenate([unit.astype(f32), rows[:, BLOCK:]], axis=1)
        split_mat()

    def send_coef(step, value):
        own_coef[step, me_b] = value
        for o in range(1, blk_count):
            piece = own_coef.at[step, me_b]
            send(None, piece, piece, cg_s.at[step, o], cg_r.at[step, o], (me_d, blk_peer(o)))

    def all_coef(step):
        for o in range(1, blk_count):
            piece = own_coef.at[step, 0]
            remote(piece, piece, cg_s.at[step, o], cg_r.at[step, o], (me_d, blk_peer(-o))).wait_recv()
        return jnp.concatenate([own_coef[step, i] for i in range(blk_count)], axis=0)

    def send_pending(step, pending):
        pend[step, me_b] = pending
        for o in range(1, blk_count):
            piece = pend.at[step, me_b]
            send(None, piece, piece, pg_s.at[step, o], pg_r.at[step, o], (me_d, blk_peer(o)))

    def send_gram(step):
        for o in range(1, blk_count):
            remote(pend.at[step, 0], pend.at[step, 0], pg_s.at[step, o], pg_r.at[step, o], (me_d, blk_peer(-o))).wait_recv()
        full = jnp.concatenate([pend[step, i] for i in range(blk_count)], axis=0)
        high, low = halves(full)
        cross = dot(high, low, NT)
        gram_part = dot(high, high, NT) + cross + cross.T
        half = BLOCK // 2
        gram_in[step, me_d] = jnp.concatenate([gram_part[:half], gram_part[half:]], axis=1)
        for o in range(1, dom_count):
            piece = gram_in.at[step, me_d]
            send(None, piece, piece, gr_s.at[step, o], gr_r.at[step, o], (dom_peer(o), me_b))

    def end_gram(step):
        for o in range(1, dom_count):
            piece = gram_in.at[step, 0]
            remote(piece, piece, gr_s.at[step, o], gr_r.at[step, o], (dom_peer(-o), me_b)).wait_recv()
        total = gram_in[step, 0]
        for d in range(1, dom_count):
            total += gram_in[step, d]
        total = total / row_total
        return jnp.concatenate([total[:, :BLOCK], total[:, BLOCK:]], axis=0)

    def summed(a, value, meanwhile):
        lanes = STORED // LANE
        for j in range(PIECES):
            h, q = divmod(j, lanes)
            part[a, j] = value[h * SUB : (h + 1) * SUB, q * LANE : (q + 1) * LANE]
        for o in range(1, dom_count):
            to = dom_peer(o)
            cond = None if all_own else to < PIECES
            piece = to if all_own else lax.rem(to, PIECES)
            send(cond, part.at[a, piece], rs_in.at[a, o], rs_s.at[a, o], rs_r.at[a, o], (to, me_b))
        meanwhile()

        def reduce():
            total = part[a, mine]
            for o in range(1, dom_count):
                remote(part.at[a, 0], rs_in.at[a, o], rs_s.at[a, o], rs_r.at[a, o], (dom_peer(-o), me_b)).wait_recv()
                total += rs_in[a, o]
            coef[a, mine] = total / row_total

        when(owner, reduce)
        for o in range(1, dom_count):
            send(owner, coef.at[a, mine], coef.at[a, mine], ag_s.at[a, o], ag_r.at[a, o], (dom_peer(o), me_b))
        for o in range(1, dom_count):
            origin = dom_peer(-o)
            cond = None if all_own else origin < PIECES
            copy = remote(coef.at[a, 0], coef.at[a, 0], ag_s.at[a, o], ag_r.at[a, o], (origin, me_b))
            when(cond, copy.wait_recv)
        return jnp.concatenate(
            [jnp.concatenate([coef[a, h * lanes + q] for q in range(lanes)], axis=1) for h in range(PIECES // lanes)], axis=0
        )

    start_halo(0, share_in[...])
    ext_b[5 * tiles] = jnp.zeros(ext_b.shape[1:], bf16)
    for t in range(tiles):
        pltpu.make_async_copy(hess_ref.at[t], hess_f.at[t], hess_sem.at[t]).wait()

        @pl.loop(0, listed)
        def _(k):
            high, low = halves(hess_f[t, k])
            hess_hi[t, k] = high
            hess_lo[t, k] = low

    split_stored(me_b)
    for step in range(STEPS):
        end_halo(step)
        product(0, tiles // 2)
        if step == 0:
            remote(basis_ref, stored_f.at[0], st_s.at[0], st_r.at[0], (me_d, across)).wait_recv()
            send(None, stored_f.at[across], stored_f.at[across], st_s.at[2], st_r.at[2], (me_d, partner))
        product(tiles // 2, tiles)
        pending = jnp.concatenate([prod[t] for t in range(tiles)], axis=1)
        if step == 0:
            split_stored(across)
            for i, origin in ((1, partner), (2, lax.rem(partner + 2, 4))):
                remote(basis_ref, stored_f.at[0], st_s.at[i], st_r.at[i], (me_d, partner)).wait_recv()
                split_stored(origin)
        if step == 0:
            for sweep, meanwhile in enumerate((scatter_mat, reduce_mat)):
                both = stacked(pending)
                inner = folded((dot(stored_hi[...], both, NT) + dot(stored_lo[...], both, NT)).T)
                coefficients = summed(sweep, inner, meanwhile)
                both = stacked(coefficients)
                pending = pending - folded(dot(both, stored_hi[...], NN) + dot(both, stored_lo[...], NN))
            send_pending(step, pending)
            send_coef(step, coefficients)
            send_gram(step)
            spread_mat()
            gram = end_gram(step)
            full = jnp.concatenate([pend[step, i] for i in range(blk_count)], axis=0)
        else:
            send_pending(step, pending)
            both = stacked(pending)
            inner = folded((dot(stored_hi[...], both, NT) + dot(stored_lo[...], both, NT)).T)
            send_coef(step, summed(SWEEPS, inner, functools.partial(send_gram, step)))
            first = all_coef(step)
            second = first - times_mat(first)
            left = second - times_mat(second)
            coefficients = first + second
            both = stacked(coefficients)
            full = jnp.concatenate([pend[step, i] for i in range(blk_count)], axis=0)
            full = full - folded(dot(both, stored_hi[...], NN) + dot(both, stored_lo[...], NN))
            gram = end_gram(step)
            gram -= lax.dot_general(coefficients, first, NT, precision=finest, preferred_element_type=f32)
            gram -= lax.dot_general(left, coefficients, NT, precision=finest, preferred_element_type=f32)
        upper, inverse = factorize(gram)
        factors_ref[step] = upper
        new = lax.dot_general(inverse, full, NN, precision=finest, preferred_element_type=f32)
        new_full[step] = new
        share = new_full[step, pl.ds(pl.multiple_of(me_b * own, own), own), :]
        blocks_ref[step] = share
        if step + 1 < STEPS:
            start_halo(step + 1, share)
            high, low = halves(new)
            stored_hi[:BLOCK] = high
            stored_lo[:BLOCK] = low
            replace_mat(inverse)

    for cond, copy in sent:
        when(cond, copy.wait_send)


def local(hessian, neighbours, counts, basis_vectors):
    dom_count = lax.axis_size("dom")
    blk_count = lax.axis_size("blk")
    me_dom = lax.axis_index("dom")
    tiles, listed, tile_rows, _ = hessian.shape
    per_blk, width = basis_vectors.shape
    own = BLOCK // blk_count
    slot = (neighbours // tiles - me_dom + 2) % dom_count * tiles + neighbours % tiles
    live = jnp.arange(listed)[None, :] < counts[:, None]
    slots = jnp.where(live, slot, 5 * tiles).reshape(-1).astype(jnp.int32)
    sums = STEPS * SWEEPS - 1
    each = per_blk // PIECES
    dma = pltpu.SemaphoreType.DMA
    vmem = pl.BlockSpec(memory_space=pltpu.VMEM)
    return pl.pallas_call(
        functools.partial(kernel, dom_count, blk_count),
        out_shape=(
            jax.ShapeDtypeStruct((STEPS, own, width), f32),
            jax.ShapeDtypeStruct((STEPS, BLOCK, BLOCK), f32),
        ),
        in_specs=[pl.BlockSpec(memory_space=pltpu.SMEM), pl.BlockSpec(memory_space=pl.ANY), vmem],
        out_specs=(vmem, vmem),
        scratch_shapes=[
            pltpu.VMEM(hessian.shape, f32),
            pltpu.VMEM(hessian.shape, bf16),
            pltpu.VMEM(hessian.shape, bf16),
            pltpu.VMEM((own, width), f32),
            pltpu.VMEM((STEPS, 5, tiles, own, tile_rows), f32),
            pltpu.VMEM((5 * tiles + 1, 2 * own, tile_rows), bf16),
            pltpu.VMEM((tiles, own, tile_rows), f32),
            pltpu.VMEM((blk_count, per_blk, width), f32),
            pltpu.VMEM((STORED, width), bf16),
            pltpu.VMEM((STORED, width), bf16),
            pltpu.VMEM((sums, PIECES, SUB, LANE), f32),
            pltpu.VMEM((sums, dom_count, SUB, LANE), f32),
            pltpu.VMEM((sums, PIECES, SUB, LANE), f32),
            pltpu.VMEM((STEPS, blk_count, own, width), f32),
            pltpu.VMEM((STEPS, dom_count, BLOCK // 2, 2 * BLOCK), f32),
            pltpu.VMEM((STEPS, BLOCK, width), f32),
            pltpu.VMEM((STEPS, blk_count, own, STORED), f32),
            pltpu.VMEM((PIECES, each, STORED), f32),
            pltpu.VMEM((dom_count, each, STORED), f32),
            pltpu.VMEM((blk_count, PIECES, each, STORED), f32),
            pltpu.VMEM((STORED, STORED), f32),
            pltpu.VMEM((STORED, STORED), bf16),
            pltpu.VMEM((STORED, STORED), bf16),
            dma((tiles,)),
            dma((blk_count,)), dma,
            dma((3,)), dma((3,)),
            dma((STEPS, 4)), dma((STEPS, 4)),
            dma((sums, dom_count)), dma((sums, dom_count)),
            dma((sums, dom_count)), dma((sums, dom_count)),
            dma((STEPS, blk_count)), dma((STEPS, blk_count)),
            dma((STEPS, dom_count)), dma((STEPS, dom_count)),
            dma((STEPS, blk_count)), dma((STEPS, blk_count)),
            dma((dom_count,)), dma((dom_count,)),
            dma((dom_count,)), dma((dom_count,)),
            dma((blk_count,)), dma((blk_count,)),
        ],
        compiler_params=pltpu.CompilerParams(
            collective_id=0, has_side_effects=True, vmem_limit_bytes=56 * 1024 * 1024
        ),
        name="lanczos",
    )(slots, hessian, basis_vectors)


def solution(mesh):
    placed = (P("dom", None, None, None), P("dom", None), P("dom"), P("blk", "dom"))
    return jax.shard_map(
        local, mesh=mesh, in_specs=placed, out_specs=(P(None, "blk", "dom"), P()), check_vma=False
    )
```

```python
import functools

import jax
import jax.numpy as jnp
from jax import lax
from jax.experimental import pallas as pl
from jax.experimental.pallas import tpu as pltpu
from jax.sharding import PartitionSpec as P

BLOCK = 64
STORED = 512
STEPS = 2
SWEEPS = 2
PIECES = 8
SUB, LANE = 8, 128
f32, bf16 = jnp.float32, jnp.bfloat16
finest = lax.Precision.HIGHEST
NT = (((1,), (1,)), ((), ()))
NN = (((1,), (0,)), ((), ()))


def halves(value):
    high = value.astype(bf16)
    return high, (value - high.astype(f32)).astype(bf16)


def stacked(value):
    return jnp.concatenate(halves(value), axis=0)


def folded(double):
    rows = double.shape[0] // 2
    return double[:rows] + double[rows:]


def dot(left, right, dims):
    return lax.dot_general(left, right, dims, preferred_element_type=f32)


def factorize(gram):
    size = gram.shape[0]
    row_id = lax.broadcasted_iota(jnp.int32, (size, size), 0)
    col_id = lax.broadcasted_iota(jnp.int32, (size, size), 1)
    both = jnp.concatenate([gram, (row_id == col_id).astype(f32)], axis=1)
    groups = [both[SUB * g : SUB * g + SUB] for g in range(size // SUB)]
    sub_id = lax.broadcasted_iota(jnp.int32, (SUB, 2 * size), 0)
    spread = (SUB, 2 * size)
    for k in range(0, size, 2):
        g, r = divmod(k, SUB)
        first = {i: jnp.broadcast_to(groups[i][:, k : k + 1], spread) for i in range(g, len(groups))}
        second = {i: jnp.broadcast_to(groups[i][:, k + 1 : k + 2], spread) for i in range(g, len(groups))}
        row0, row1 = groups[g][r : r + 1], groups[g][r + 1 : r + 2]
        inverse0 = 1.0 / first[g][r : r + 1]
        below = first[g][r + 1 : r + 2]
        scale = below * inverse0
        inverse1 = 1.0 / (second[g][r + 1 : r + 2] - scale * below)
        row1 = row1 - scale * row0
        solved1 = row1 * inverse1
        solved0 = row0 * inverse0 - scale * solved1
        for i in range(g, len(groups)):
            rest = groups[i] - first[i] * solved0 - second[i] * solved1
            if i == g:
                rest = jnp.where(sub_id > r + 1, rest, jnp.where(sub_id == r + 1, row1, groups[i]))
            groups[i] = rest
    both = jnp.concatenate(groups, axis=0)
    upper = both[:, :size]
    diagonal = jnp.sum(jnp.where(row_id == col_id, upper, 0.0), axis=1, keepdims=True)
    both = both * lax.rsqrt(diagonal)
    return jnp.where(col_id >= row_id, both[:, :size], 0.0), both[:, size:]


def kernel(
    dom_count, blk_count,
    slots_ref, hess_ref, basis_ref,
    blocks_ref, factors_ref,
    hess_f, hess_hi, hess_lo, share_in, ext, ext_b, prod, stored_f, stored_hi, stored_lo,
    part, rs_in, coef, pend, gram_in, new_full, own_coef, mat_part, mat_in, mat_all, mat, mat_hi, mat_lo,
    hess_sem, x_s, x_r, st_s, st_r, halo_s, halo_r, rs_s, rs_r, ag_s, ag_r, pg_s, pg_r, gr_s, gr_r,
    cg_s, cg_r, ms_s, ms_r, mg_s, mg_r, mb_s, mb_r,
):
    tiles, listed, tile_rows, _ = hess_ref.shape
    per_blk, width = basis_ref.shape
    own = BLOCK // blk_count
    row_total = width * dom_count
    me_d, me_b = lax.axis_index("dom"), lax.axis_index("blk")
    sent = []

    def when(cond, do):
        if cond is None:
            do()
        else:
            pl.when(cond)(do)

    def remote(src, dst, send, recv, target):
        return pltpu.make_async_remote_copy(
            src_ref=src, dst_ref=dst, send_sem=send, recv_sem=recv,
            device_id=target, device_id_type=pl.DeviceIdType.MESH,
        )

    def send(cond, *what):
        copy = remote(*what)
        when(cond, copy.start)
        sent.append((cond, copy))

    for t in range(tiles):
        pltpu.make_async_copy(hess_ref.at[t], hess_f.at[t], hess_sem.at[t]).start()

    def dom_peer(o):
        return lax.rem(me_d + o + dom_count, dom_count)

    def blk_peer(o):
        return lax.rem(me_b + o + blk_count, blk_count)

    barrier = pltpu.get_barrier_semaphore()
    for o in range(1, dom_count):
        pl.semaphore_signal(barrier, inc=1, device_id=(dom_peer(o), me_b), device_id_type=pl.DeviceIdType.MESH)
    for o in range(1, blk_count):
        pl.semaphore_signal(barrier, inc=1, device_id=(me_d, blk_peer(o)), device_id_type=pl.DeviceIdType.MESH)
    pl.semaphore_wait(barrier, dom_count + blk_count - 2)

    last = blk_count - 1
    for j in range(last):
        rows = basis_ref.at[pl.ds(per_blk - BLOCK + own * j, own)]
        send(me_b == last, rows, share_in, x_s.at[j], x_r, (me_d, j))

    partner = me_b + 1 - 2 * lax.rem(me_b, 2)
    across = lax.rem(me_b + 2, 4)
    send(None, basis_ref, stored_f.at[me_b], st_s.at[0], st_r.at[0], (me_d, across))
    send(None, basis_ref, stored_f.at[me_b], st_s.at[1], st_r.at[1], (me_d, partner))
    stored_f[me_b] = basis_ref[...]

    @pl.when(me_b == last)
    def _():
        share_in[...] = basis_ref[per_blk - own :, :]

    @pl.when(me_b != last)
    def _():
        remote(share_in, share_in, x_s.at[0], x_r, (me_d, last)).wait_recv()

    def start_halo(step, share):
        for t in range(tiles):
            ext[step, 2, t] = share[:, t * tile_rows : (t + 1) * tile_rows]
        for i, o in enumerate((2, -2, 1, -1)):
            send(None, ext.at[step, 2], ext.at[step, 2 - o], halo_s.at[step, i], halo_r.at[step, i], (dom_peer(o), me_b))

    def split_ext(step, i):
        for t in range(tiles):
            ext_b[i * tiles + t] = stacked(ext[step, i, t])

    def end_halo(step):
        split_ext(step, 2)
        for i, o in enumerate((2, -2, 1, -1)):
            remote(ext.at[step, 2], ext.at[step, 2 - o], halo_s.at[step, i], halo_r.at[step, i], (dom_peer(-o), me_b)).wait_recv()
            split_ext(step, 2 - o)

    def product(first, end):
        @pl.loop(first, end)
        def _(t):
            total = jnp.zeros((tile_rows, 2 * own), f32)
            for k in range(listed):
                x = ext_b[slots_ref[t * listed + k]]
                total += dot(hess_hi[t, k], x, NT) + dot(hess_lo[t, k], x, NT)
            prod[t] = folded(total.T)

    def split_stored(i):
        high, low = halves(stored_f[i])
        rows = pl.ds(pl.multiple_of(i * per_blk, per_blk), per_blk)
        stored_hi[rows] = high
        stored_lo[rows] = low

    all_own = dom_count <= PIECES
    mine = me_d if all_own else lax.rem(me_d, PIECES)
    owner = None if all_own else me_d < PIECES

    def scatter_mat():
        rows = pl.ds(pl.multiple_of(me_b * per_blk, per_blk), per_blk)
        high, low = stored_hi[rows], stored_lo[rows]
        value = dot(high, stored_hi[...], NT) + dot(high, stored_lo[...], NT) + dot(low, stored_hi[...], NT)
        each = per_blk // PIECES
        for j in range(PIECES):
            mat_part[j] = value[j * each : (j + 1) * each]
        for o in range(1, dom_count):
            to = dom_peer(o)
            cond = None if all_own else to < PIECES
            piece = to if all_own else lax.rem(to, PIECES)
            send(cond, mat_part.at[piece], mat_in.at[o], ms_s.at[o], ms_r.at[o], (to, me_b))

    def reduce_mat():
        def reduce():
            total = mat_part[mine]
            for o in range(1, dom_count):
                remote(mat_part.at[0], mat_in.at[o], ms_s.at[o], ms_r.at[o], (dom_peer(-o), me_b)).wait_recv()
                total += mat_in[o]
            mat_all[me_b, mine] = total / row_total

        when(owner, reduce)
        for o in range(1, dom_count):
            piece = mat_all.at[me_b, mine]
            send(owner, piece, piece, mg_s.at[o], mg_r.at[o], (dom_peer(o), me_b))

    def spread_mat():
        for o in range(1, dom_count):
            origin = dom_peer(-o)
            cond = None if all_own else origin < PIECES
            piece = mat_all.at[me_b, 0]
            when(cond, remote(piece, piece, mg_s.at[o], mg_r.at[o], (origin, me_b)).wait_recv)
        for o in range(1, blk_count):
            send(None, mat_all.at[me_b], mat_all.at[me_b], mb_s.at[o], mb_r.at[o], (me_d, blk_peer(o)))

    def times_mat(value):
        both = stacked(value)
        return folded(dot(both, mat_hi[...], NN) + dot(both, mat_lo[...], NN))

    def split_mat():
        high, low = halves(mat[...])
        mat_hi[...] = high
        mat_lo[...] = low

    def replace_mat(inverse):
        for o in range(1, blk_count):
            remote(mat_all.at[0], mat_all.at[0], mb_s.at[o], mb_r.at[o], (me_d, blk_peer(-o))).wait_recv()
        each = per_blk // PIECES
        for i in range(blk_count):
            for j in range(PIECES):
                mat[i * per_blk + j * each : i * per_blk + (j + 1) * each] = mat_all[i, j]
        split_mat()
        second = all_coef(0)
        rows = lax.dot_general(
            inverse, second - times_mat(second), NN, precision=finest, preferred_element_type=f32
        )
        mat[:, : 2 * BLOCK] = jnp.concatenate([rows.T, mat[:, BLOCK : 2 * BLOCK]], axis=1)
        unit = lax.broadcasted_iota(jnp.int32, (BLOCK, BLOCK), 0) == lax.broadcasted_iota(jnp.int32, (BLOCK, BLOCK), 1)
        mat[:BLOCK] = jnp.concatenate([unit.astype(f32), rows[:, BLOCK:]], axis=1)
        split_mat()

    def send_coef(step, value):
        own_coef[step, me_b] = value
        for o in range(1, blk_count):
            piece = own_coef.at[step, me_b]
            send(None, piece, piece, cg_s.at[step, o], cg_r.at[step, o], (me_d, blk_peer(o)))

    def all_coef(step):
        for o in range(1, blk_count):
            piece = own_coef.at[step, 0]
            remote(piece, piece, cg_s.at[step, o], cg_r.at[step, o], (me_d, blk_peer(-o))).wait_recv()
        return jnp.concatenate([own_coef[step, i] for i in range(blk_count)], axis=0)

    def send_pending(step, pending):
        pend[step, me_b] = pending
        for o in range(1, blk_count):
            piece = pend.at[step, me_b]
            send(None, piece, piece, pg_s.at[step, o], pg_r.at[step, o], (me_d, blk_peer(o)))

    def send_gram(step):
        for o in range(1, blk_count):
            remote(pend.at[step, 0], pend.at[step, 0], pg_s.at[step, o], pg_r.at[step, o], (me_d, blk_peer(-o))).wait_recv()
        full = jnp.concatenate([pend[step, i] for i in range(blk_count)], axis=0)
        high, low = halves(full)
        cross = dot(high, low, NT)
        gram_part = dot(high, high, NT) + cross + cross.T
        half = BLOCK // 2
        gram_in[step, me_d] = jnp.concatenate([gram_part[:half], gram_part[half:]], axis=1)
        for o in range(1, dom_count):
            piece = gram_in.at[step, me_d]
            send(None, piece, piece, gr_s.at[step, o], gr_r.at[step, o], (dom_peer(o), me_b))

    def end_gram(step):
        for o in range(1, dom_count):
            piece = gram_in.at[step, 0]
            remote(piece, piece, gr_s.at[step, o], gr_r.at[step, o], (dom_peer(-o), me_b)).wait_recv()
        total = gram_in[step, 0]
        for d in range(1, dom_count):
            total += gram_in[step, d]
        total = total / row_total
        return jnp.concatenate([total[:, :BLOCK], total[:, BLOCK:]], axis=0)

    def summed(a, value, meanwhile, later=None):
        lanes = STORED // LANE
        for j in range(PIECES):
            h, q = divmod(j, lanes)
            part[a, j] = value[h * SUB : (h + 1) * SUB, q * LANE : (q + 1) * LANE]
        for o in range(1, dom_count):
            to = dom_peer(o)
            cond = None if all_own else to < PIECES
            piece = to if all_own else lax.rem(to, PIECES)
            send(cond, part.at[a, piece], rs_in.at[a, o], rs_s.at[a, o], rs_r.at[a, o], (to, me_b))
        meanwhile()

        def reduce():
            total = part[a, mine]
            for o in range(1, dom_count):
                remote(part.at[a, 0], rs_in.at[a, o], rs_s.at[a, o], rs_r.at[a, o], (dom_peer(-o), me_b)).wait_recv()
                total += rs_in[a, o]
            coef[a, mine] = total / row_total

        when(owner, reduce)
        for o in range(1, dom_count):
            send(owner, coef.at[a, mine], coef.at[a, mine], ag_s.at[a, o], ag_r.at[a, o], (dom_peer(o), me_b))
        if later is not None:
            later()
        for o in range(1, dom_count):
            origin = dom_peer(-o)
            cond = None if all_own else origin < PIECES
            copy = remote(coef.at[a, 0], coef.at[a, 0], ag_s.at[a, o], ag_r.at[a, o], (origin, me_b))
            when(cond, copy.wait_recv)
        return jnp.concatenate(
            [jnp.concatenate([coef[a, h * lanes + q] for q in range(lanes)], axis=1) for h in range(PIECES // lanes)], axis=0
        )

    start_halo(0, share_in[...])
    ext_b[5 * tiles] = jnp.zeros(ext_b.shape[1:], bf16)
    for t in range(tiles):
        pltpu.make_async_copy(hess_ref.at[t], hess_f.at[t], hess_sem.at[t]).wait()

        @pl.loop(0, listed)
        def _(k):
            high, low = halves(hess_f[t, k])
            hess_hi[t, k] = high
            hess_lo[t, k] = low

    split_stored(me_b)
    for step in range(STEPS):
        end_halo(step)
        product(0, tiles // 2)
        if step == 0:
            remote(basis_ref, stored_f.at[0], st_s.at[0], st_r.at[0], (me_d, across)).wait_recv()
            send(None, stored_f.at[across], stored_f.at[across], st_s.at[2], st_r.at[2], (me_d, partner))
        product(tiles // 2, tiles)
        pending = jnp.concatenate([prod[t] for t in range(tiles)], axis=1)
        if step == 0:
            split_stored(across)
            for i, origin in ((1, partner), (2, lax.rem(partner + 2, 4))):
                remote(basis_ref, stored_f.at[0], st_s.at[i], st_r.at[i], (me_d, partner)).wait_recv()
                split_stored(origin)
        if step == 0:
            for sweep, meanwhile in enumerate((scatter_mat, reduce_mat)):
                both = stacked(pending)
                inner = folded((dot(stored_hi[...], both, NT) + dot(stored_lo[...], both, NT)).T)
                coefficients = summed(sweep, inner, meanwhile)
                both = stacked(coefficients)
                pending = pending - folded(dot(both, stored_hi[...], NN) + dot(both, stored_lo[...], NN))
            send_pending(step, pending)
            send_coef(step, coefficients)
            send_gram(step)
            spread_mat()
            gram = end_gram(step)
            full = jnp.concatenate([pend[step, i] for i in range(blk_count)], axis=0)
        else:
            send_pending(step, pending)
            both = stacked(pending)
            inner = folded((dot(stored_hi[...], both, NT) + dot(stored_lo[...], both, NT)).T)
            send_gram_later = functools.partial(send_gram, step)
            send_coef(step, summed(SWEEPS, inner, send_gram_later, functools.partial(replace_mat, inverse)))
            first = all_coef(step)
            second = first - times_mat(first)
            left = second - times_mat(second)
            coefficients = first + second
            both = stacked(coefficients)
            full = jnp.concatenate([pend[step, i] for i in range(blk_count)], axis=0)
            full = full - folded(dot(both, stored_hi[...], NN) + dot(both, stored_lo[...], NN))
            gram = end_gram(step)
            gram -= lax.dot_general(coefficients, first, NT, precision=finest, preferred_element_type=f32)
            gram -= lax.dot_general(left, coefficients, NT, precision=finest, preferred_element_type=f32)
        upper, inverse = factorize(gram)
        factors_ref[step] = upper
        new = lax.dot_general(inverse, full, NN, precision=finest, preferred_element_type=f32)
        new_full[step] = new
        share = new_full[step, pl.ds(pl.multiple_of(me_b * own, own), own), :]
        blocks_ref[step] = share
        if step + 1 < STEPS:
            start_halo(step + 1, share)
            high, low = halves(new)
            stored_hi[:BLOCK] = high
            stored_lo[:BLOCK] = low

    for cond, copy in sent:
        when(cond, copy.wait_send)


def local(hessian, neighbours, counts, basis_vectors):
    dom_count = lax.axis_size("dom")
    blk_count = lax.axis_size("blk")
    me_dom = lax.axis_index("dom")
    tiles, listed, tile_rows, _ = hessian.shape
    per_blk, width = basis_vectors.shape
    own = BLOCK // blk_count
    slot = (neighbours // tiles - me_dom + 2) % dom_count * tiles + neighbours % tiles
    live = jnp.arange(listed)[None, :] < counts[:, None]
    slots = jnp.where(live, slot, 5 * tiles).reshape(-1).astype(jnp.int32)
    sums = STEPS * SWEEPS - 1
    each = per_blk // PIECES
    dma = pltpu.SemaphoreType.DMA
    vmem = pl.BlockSpec(memory_space=pltpu.VMEM)
    return pl.pallas_call(
        functools.partial(kernel, dom_count, blk_count),
        out_shape=(
            jax.ShapeDtypeStruct((STEPS, own, width), f32),
            jax.ShapeDtypeStruct((STEPS, BLOCK, BLOCK), f32),
        ),
        in_specs=[pl.BlockSpec(memory_space=pltpu.SMEM), pl.BlockSpec(memory_space=pl.ANY), vmem],
        out_specs=(vmem, vmem),
        scratch_shapes=[
            pltpu.VMEM(hessian.shape, f32),
            pltpu.VMEM(hessian.shape, bf16),
            pltpu.VMEM(hessian.shape, bf16),
            pltpu.VMEM((own, width), f32),
            pltpu.VMEM((STEPS, 5, tiles, own, tile_rows), f32),
            pltpu.VMEM((5 * tiles + 1, 2 * own, tile_rows), bf16),
            pltpu.VMEM((tiles, own, tile_rows), f32),
            pltpu.VMEM((blk_count, per_blk, width), f32),
            pltpu.VMEM((STORED, width), bf16),
            pltpu.VMEM((STORED, width), bf16),
            pltpu.VMEM((sums, PIECES, SUB, LANE), f32),
            pltpu.VMEM((sums, dom_count, SUB, LANE), f32),
            pltpu.VMEM((sums, PIECES, SUB, LANE), f32),
            pltpu.VMEM((STEPS, blk_count, own, width), f32),
            pltpu.VMEM((STEPS, dom_count, BLOCK // 2, 2 * BLOCK), f32),
            pltpu.VMEM((STEPS, BLOCK, width), f32),
            pltpu.VMEM((STEPS, blk_count, own, STORED), f32),
            pltpu.VMEM((PIECES, each, STORED), f32),
            pltpu.VMEM((dom_count, each, STORED), f32),
            pltpu.VMEM((blk_count, PIECES, each, STORED), f32),
            pltpu.VMEM((STORED, STORED), f32),
            pltpu.VMEM((STORED, STORED), bf16),
            pltpu.VMEM((STORED, STORED), bf16),
            dma((tiles,)),
            dma((blk_count,)), dma,
            dma((3,)), dma((3,)),
            dma((STEPS, 4)), dma((STEPS, 4)),
            dma((sums, dom_count)), dma((sums, dom_count)),
            dma((sums, dom_count)), dma((sums, dom_count)),
            dma((STEPS, blk_count)), dma((STEPS, blk_count)),
            dma((STEPS, dom_count)), dma((STEPS, dom_count)),
            dma((STEPS, blk_count)), dma((STEPS, blk_count)),
            dma((dom_count,)), dma((dom_count,)),
            dma((dom_count,)), dma((dom_count,)),
            dma((blk_count,)), dma((blk_count,)),
        ],
        compiler_params=pltpu.CompilerParams(
            collective_id=0, has_side_effects=True, vmem_limit_bytes=56 * 1024 * 1024
        ),
        name="lanczos",
    )(slots, hessian, basis_vectors)


def solution(mesh):
    placed = (P("dom", None, None, None), P("dom", None), P("dom"), P("blk", "dom"))
    return jax.shard_map(
        local, mesh=mesh, in_specs=placed, out_specs=(P(None, "blk", "dom"), P()), check_vma=False
    )
```
